32 devices in a mesh: dp: 8 (over y, x, core), tensor: 4 (over z).
Axes of the slice: x: 2, y: 2, z: 4, core: 2. Of those that a mesh axis runs over, the one named last changes fastest.
Arguments:
- tokens: bfloat16 [3072, 2048], P('dp'), may hold values from -6 to 6
- out_grad: bfloat16 [3072, 7168], P('dp', 'tensor'), may hold values from -6 to 6
- gate_weight: bfloat16 [2048, 7168], P('dp', 'tensor'), may hold values from -0.1875 to 0.1875
- up_weight: bfloat16 [2048, 7168], P('dp', 'tensor'), may hold values from -0.1875 to 0.1875
- gate_mask: int32 [32, 112], P('dp', 'tensor'), may hold values 0 or 1
- up_mask: int32 [32, 112], P('dp', 'tensor'), may hold values 0 or 1
Outputs:
- hidden: float32 [3072, 7168], P('dp', 'tensor')
- grad_tokens: bfloat16 [3072, 2048], P('dp')
- grad_gate: float32 [2048, 7168], P('dp', 'tensor')
- grad_up: float32 [2048, 7168], P('dp', 'tensor')
The draws below stay inside these ranges and needn't reach their ends.
All inputs are finite; a program needn't handle non-finite values. No bound on the sum of `gate_mask` or of `up_mask` on one device may be relied on, other than what follows from the above.
Results may differ from the reference program's by a relative error of at most 0.014.
Values may be sent and summed in bfloat16 or wider, within the bound.
A program may use at most 128 MiB of HBM per device.

```python
import jax
import jax.numpy as jnp
from jax import lax

D = 2048
FF = 7168
BLOCK = 64
TOK_GROUP = 384
TOKENS = 3072
N_DP = 8


def touch_ends(drawn, rng, least, high):
    spot = [jax.random.randint(jax.random.fold_in(rng, axis), (), 0, length) for axis, length in enumerate(drawn.shape)]
    longest = drawn.shape.index(max(drawn.shape))
    beside = spot[:longest] + [(spot[longest] + 1) % drawn.shape[longest]] + spot[longest + 1:]
    return drawn.at[tuple(spot)].set(least).at[tuple(beside)].set(high)


def with_spikes(array, own_key, source, target, blocks, factor):
    def block_of(axis_at):
        return (jnp.arange(array.shape[axis_at]) // (array.shape[axis_at] // blocks)).reshape((-1,) + (1,) * (array.ndim - 1 - axis_at))

    near = jax.random.permutation(own_key, blocks)[block_of(target)]
    other_side = (block_of(target) + blocks // 2) % blocks
    return jnp.where((block_of(source) == near) | (block_of(source) == other_side), factor * array, array)


def shard_levels(key, dims, cuts, low, top_value):
    level = 1.0
    for position, parts in cuts:
        steps = jax.random.uniform(jax.random.fold_in(jax.random.fold_in(key, 6), position), (parts,), jnp.float32, low / len(cuts), top_value / len(cuts))
        level = level * jnp.repeat(jnp.exp(steps), dims[position] // parts).reshape((-1,) + (1,) * (len(dims) - 1 - position))
    return level


def bell_draw(own_key, extent, deviation, most, cuts=(), held_as=jnp.bfloat16):
    level = shard_levels(own_key, extent, cuts, -0.22, 0.18) if cuts else 1.0
    result = jax.random.normal(own_key, extent, jnp.float32) * deviation * level
    return jnp.minimum(jnp.maximum(result, -most), most).astype(held_as)


def noise_with(own_key, dims, deviation, most, split, heavy, dtype=jnp.bfloat16):
    entries = deviation * jax.random.normal(own_key, dims, jnp.float32)
    if split:
        entries = entries * shard_levels(own_key, dims, split, -0.22, 0.18)
    return jnp.clip(with_spikes(entries, jax.random.fold_in(own_key, 3), *heavy), -most, most).astype(dtype)


def setup_inputs(seed: int = 0) -> dict:
    arg_keys = jax.random.split(jax.random.key(seed), 7)
    tokens = noise_with(arg_keys[0], (TOKENS, D), 1.0, 6.0, ((0, 8),), (0, 1, 8, 2.0))
    out_grad = bell_draw(arg_keys[1], (TOKENS, FF), 1.0, 6.0, ((0, 8), (1, 4)))
    gate_weight = bell_draw(arg_keys[2], (D, FF), (D // 2) ** -0.5, 0.1875, ((0, 8), (1, 4)))
    up_weight = bell_draw(arg_keys[3], (D, FF), (D // 2) ** -0.5, 0.1875, ((0, 8), (1, 4)))
    gate_mask = touch_ends((jax.random.randint(arg_keys[4], (D // BLOCK, FF // BLOCK), 0, 2) < 1).astype(jnp.int32), jax.random.fold_in(arg_keys[4], 1), 0, 1)
    up_mask = touch_ends((jax.random.randint(arg_keys[5], (D // BLOCK, FF // BLOCK), 0, 2) < 1).astype(jnp.int32), jax.random.fold_in(arg_keys[5], 1), 0, 1)
    return {"tokens": tokens, "out_grad": out_grad, "gate_weight": gate_weight, "up_weight": up_weight, "gate_mask": gate_mask, "up_mask": up_mask}


def expand(block_mask):
    height, breadth = block_mask.shape
    values = block_mask.astype(jnp.float32)
    return jnp.broadcast_to(values[:, None, :, None], (height, BLOCK, breadth, BLOCK)).reshape(height * BLOCK, breadth * BLOCK)


def reference(tokens, out_grad, gate_weight, up_weight, gate_mask, up_mask):
    gate_keep = expand(gate_mask)
    up_keep = expand(up_mask)
    gate_eff = (gate_weight.astype(jnp.float32) * gate_keep).astype(jnp.bfloat16)
    up_eff = (up_weight.astype(jnp.float32) * up_keep).astype(jnp.bfloat16)
    both_eff = jnp.concatenate([gate_eff, up_eff], axis=1)
    token_groups = tokens.reshape(N_DP, TOK_GROUP, D)
    grad_groups = out_grad.reshape(N_DP, TOK_GROUP, FF)

    def group_step(grad_total, operands):
        group_tokens, group_grad = operands
        preact = jnp.dot(group_tokens, both_eff, preferred_element_type=jnp.float32)
        gate = preact[:, :FF]
        up = preact[:, FF:]
        sigmoid_gate = jax.nn.sigmoid(gate)
        activation = gate * sigmoid_gate
        hidden = activation * up
        grad_float = group_grad.astype(jnp.float32)
        d_gate = (grad_float * up * sigmoid_gate * (1.0 + gate * (1.0 - sigmoid_gate))).astype(jnp.bfloat16)
        d_up = (grad_float * activation).astype(jnp.bfloat16)
        d_both = jnp.concatenate([d_gate, d_up], axis=1)
        input_grad = lax.dot_general(d_both, both_eff, (((1,), (1,)), ((), ())), preferred_element_type=jnp.float32).astype(jnp.bfloat16)
        partial_rows = lax.dot_general(group_tokens, d_both, (((0,), (0,)), ((), ())), preferred_element_type=jnp.float32).astype(jnp.bfloat16)
        partial_rows = lax.optimization_barrier(partial_rows)
        grad_total = grad_total + partial_rows.astype(jnp.float32)
        return grad_total, (hidden, input_grad)

    grad_total, (hidden_all, input_all) = lax.scan(group_step, jnp.zeros((D, 2 * FF), jnp.float32), (token_groups, grad_groups))
    grad_gate = grad_total[:, :FF] * gate_keep
    grad_up = grad_total[:, FF:] * up_keep
    return hidden_all.reshape(TOKENS, FF), input_all.reshape(TOKENS, D), grad_gate, grad_up
```

```python
import functools

import jax
import jax.numpy as jnp
from jax import lax
from jax.experimental import pallas as pl
from jax.experimental.pallas import tpu as pltpu
from jax.sharding import PartitionSpec as P

MESH_ID = pl.DeviceIdType.MESH
F32 = jnp.float32
BF16 = jnp.bfloat16
LEAD = 3


def expand(block_mask, rows, columns):
    height, breadth = block_mask.shape
    down, across = rows // height, columns // breadth
    values = block_mask.astype(F32)
    return jnp.broadcast_to(
        values[:, None, :, None], (height, down, breadth, across)
    ).reshape(rows, columns)


def local_collective(tokens, out_grad, gate_weight, up_weight, gate_mask, up_mask):
    gate_keep = expand(gate_mask, *gate_weight.shape)
    up_keep = expand(up_mask, *up_weight.shape)
    gate_eff = gate_weight * gate_keep.astype(BF16)
    up_eff = up_weight * up_keep.astype(BF16)
    local_both = jnp.concatenate([gate_eff, up_eff], axis=1)
    hidden_width = gate_weight.shape[1]
    gathered = lax.all_gather(local_both, "dp", axis=0, tiled=True)
    preact = jnp.dot(tokens, gathered, preferred_element_type=F32)
    gate = preact[:, :hidden_width]
    up = preact[:, hidden_width:]
    sigmoid_gate = jax.nn.sigmoid(gate)
    activation = gate * sigmoid_gate
    hidden = activation * up
    grad_float = out_grad.astype(F32)
    d_gate = (grad_float * up * sigmoid_gate * (1.0 + gate * (1.0 - sigmoid_gate))).astype(BF16)
    d_up = (grad_float * activation).astype(BF16)
    d_both = jnp.concatenate([d_gate, d_up], axis=1)
    partial_input = lax.dot_general(
        d_both, gathered, (((1,), (1,)), ((), ())), preferred_element_type=F32
    )
    grad_tokens = lax.psum(partial_input, "tensor").astype(BF16)
    summed = lax.psum_scatter(
        lax.dot_general(
            tokens, d_both, (((0,), (0,)), ((), ())), preferred_element_type=F32
        ).astype(BF16),
        "dp",
        scatter_dimension=0,
        tiled=True,
    ).astype(F32)
    grad_gate = summed[:, :hidden_width] * gate_keep
    grad_up = summed[:, hidden_width:] * up_keep
    return (hidden, grad_tokens, grad_gate, grad_up)


def kernel(
    n_t, chunks, width, mask_rows,
    tok, og, gw, uw, gm, um,
    hidden, gt, ggrad, ugrad,
    wbuf, mr, xr, yr, r2, tokt, pre, dch, acc, zs, zr,
    ag_s, ag_r, ms_s, ms_r, rs_s, rs_r, z_s, z_r, za_s, za_r,
):
    rows = gw.shape[0]
    half = rows // 2
    n_tok, depth = tok.shape
    n_dp = depth // rows
    d = lax.axis_index("dp")
    t = lax.axis_index("tensor")
    c = lax.rem(d, 2)
    x = lax.rem(d // 2, 2)
    y = d // 4
    mate = d + 1 - 2 * c
    xn = d + 2 - 4 * x
    yn = d + 4 - 8 * y
    dg = xn + 4 - 8 * y

    barrier = pltpu.get_barrier_semaphore()
    for peer in (mate, xn, yn):
        pl.semaphore_signal(barrier, inc=1, device_id=(peer, t), device_id_type=MESH_ID)
    for k in range(1, n_t):
        pl.semaphore_signal(
            barrier, inc=1, device_id=(d, lax.rem(t + k, n_t)), device_id_type=MESH_ID
        )

    def at(j, block, off=0, size=rows):
        return wbuf.at[j, pl.ds(pl.multiple_of(block * rows + off, half), size)]

    def ag(kind, j):
        block, off, size, dev = (
            (d, 0, rows, xn),
            (d, 0, rows, yn),
            (xn, 0, half, yn),
            (yn, half, half, xn),
            (d, 0, rows, mate),
            (xn, 0, rows, mate),
            (yn, 0, rows, mate),
            (dg, 0, rows, mate),
        )[kind]
        return pltpu.make_async_remote_copy(
            src_ref=at(j, block, off, size), dst_ref=at(j, block, off, size),
            send_sem=ag_s.at[kind, j], recv_sem=ag_r.at[kind, j],
            device_id=(dev, t), device_id_type=MESH_ID,
        )

    def ag_in(kind, j):
        m = mate
        block, off, size = (
            (xn, 0, rows), (yn, 0, rows), (dg, 0, half), (dg, half, half),
            (m, 0, rows), (xn + m - d, 0, rows), (yn + m - d, 0, rows), (dg + m - d, 0, rows),
        )[kind]
        return pltpu.make_async_remote_copy(
            src_ref=at(j, block, off, size), dst_ref=at(j, block, off, size),
            send_sem=ag_s.at[kind, j], recv_sem=ag_r.at[kind, j],
            device_id=(mate, t), device_id_type=MESH_ID,
        )

    def ms(q, j):
        return pltpu.make_async_remote_copy(
            src_ref=at(j, 2 * q + 1 - c), dst_ref=mr.at[j, q],
            send_sem=ms_s.at[q, j], recv_sem=ms_r.at[q, j],
            device_id=(mate, t), device_id_type=MESH_ID,
        )

    def rs(kind, j):
        block, off, dst, dev = (
            (dg, 0, xr.at[j, 1], xn),
            (dg, half, yr.at[j, 1], yn),
            (xn, 0, xr.at[j, 0], xn),
            (yn, half, yr.at[j, 0], yn),
            (yn, 0, r2.at[j, 0], yn),
            (xn, half, r2.at[j, 1], xn),
        )[kind]
        return pltpu.make_async_remote_copy(
            src_ref=at(j, block, off, half), dst_ref=dst,
            send_sem=rs_s.at[kind, j], recv_sem=rs_r.at[kind, j],
            device_id=(dev, t), device_id_type=MESH_ID,
        )

    def cols(j):
        return pl.ds(pl.multiple_of(j * width, width), width)

    def keep(ref, j):
        down = rows // mask_rows
        return jnp.concatenate(
            [jnp.broadcast_to(ref[i:i + 1, cols(j)], (down, width)) for i in range(mask_rows)],
            axis=0,
        )

    def prepare(j):
        own = pl.ds(pl.multiple_of(d * rows, rows), rows)
        wbuf[j, own, :width] = (gw[:, cols(j)].astype(F32) * keep(gm, j)).astype(BF16)
        wbuf[j, own, width:] = (uw[:, cols(j)].astype(F32) * keep(um, j)).astype(BF16)

    def send_own(j):
        ag(0, j).start()
        ag(1, j).start()
        ag(4, j).start()

    lax.fori_loop(0, chunks, lambda j, u: (prepare(j), u)[1], 0)
    pl.semaphore_wait(barrier, 3 + n_t - 1)
    lead = min(LEAD, chunks)
    lax.fori_loop(0, lead, lambda j, u: (send_own(j), u)[1], 0)

    tokt[...] = tok[...].T
    acc[...] = jnp.zeros_like(acc)

    def relay(j):
        ag_in(0, j).wait_recv()
        ag(2, j).start()
        ag(5, j).start()
        ag_in(1, j).wait_recv()
        ag(3, j).start()
        ag(6, j).start()

        @pl.when(j + lead < chunks)
        def _():
            send_own(j + lead)

    def relay_far(j):
        ag_in(2, j).wait_recv()
        ag_in(3, j).wait_recv()
        ag(7, j).start()

    def compute(j):
        for kind in (4, 5, 6, 7):
            ag_in(kind, j).wait_recv()
        pre[...] = jnp.dot(tok[...], wbuf[j], preferred_element_type=F32)
        step = n_tok // 3 if n_tok % 48 == 0 else n_tok
        for i in range(0, n_tok, step):
            part = slice(i, i + step)
            gate = pre[part, :width]
            up = pre[part, width:]
            s = jax.nn.sigmoid(gate)
            activation = gate * s
            hidden[part, cols(j)] = activation * up
            g = og[part, cols(j)].astype(F32)
            dch[part, :width] = (g * up * s * (1.0 + gate * (1.0 - s))).astype(BF16)
            dch[part, width:] = (g * activation).astype(BF16)
        for b in range(n_dp):
            acc[:, b * rows:(b + 1) * rows] += lax.dot_general(
                dch[...], wbuf[j, b * rows:(b + 1) * rows, :],
                (((1,), (1,)), ((), ())), preferred_element_type=F32,
            )
        for kind in range(8):
            ag(kind, j).wait_send()
        for q in range(n_dp // 2):
            other = pl.ds(pl.multiple_of((2 * q + 1 - c) * rows, rows), rows)
            wbuf[j, other] = jnp.dot(
                tokt[other], dch[...], preferred_element_type=F32
            ).astype(BF16)
            ms(q, j).start()
        for q in range(n_dp // 2):
            mine = pl.ds(pl.multiple_of((2 * q + c) * rows, rows), rows)
            wbuf[j, mine] = jnp.dot(
                tokt[mine], dch[...], preferred_element_type=F32
            ).astype(BF16)

    def pair_sum(j):
        for q in range(n_dp // 2):
            mine = pl.ds(pl.multiple_of((2 * q + c) * rows, rows), rows)
            ms(q, j).wait_recv()
            wbuf[j, mine] = (wbuf[j, mine].astype(F32) + mr[j, q].astype(F32)).astype(BF16)
        for kind in range(4):
            rs(kind, j).start()

    def cross_sum(j):
        far = pl.ds(pl.multiple_of(yn * rows, rows), half)
        rs(0, j).wait_recv()
        wbuf[j, far] = (wbuf[j, far].astype(F32) + xr[j, 1].astype(F32)).astype(BF16)
        rs(4, j).start()
        far = pl.ds(pl.multiple_of(xn * rows + half, half), half)
        rs(1, j).wait_recv()
        wbuf[j, far] = (wbuf[j, far].astype(F32) + yr[j, 1].astype(F32)).astype(BF16)
        rs(5, j).start()

    def finish(j):
        for kind in (2, 3, 4, 5):
            rs(kind, j).wait_recv()
        for k, near in ((0, xr), (1, yr)):
            own = pl.ds(pl.multiple_of(d * rows + k * half, half), half)
            total = wbuf[j, own].astype(F32) + near[j, 0].astype(F32) + r2[j, k].astype(F32)
            part = slice(k * half, (k + 1) * half)
            ggrad[part, cols(j)] = total[:, :width] * keep(gm, j)[part]
            ugrad[part, cols(j)] = total[:, width:] * keep(um, j)[part]

    def drain(j):
        for q in range(n_dp // 2):
            ms(q, j).wait_send()
        for kind in range(6):
            rs(kind, j).wait_send()

    def when(stage, j):
        @pl.when(jnp.logical_and(j >= 0, j < chunks))
        def _():
            stage(j)

    def step(s, u):
        when(relay, s)
        when(relay_far, s - 1)
        when(compute, s - 2)
        when(pair_sum, s - 3)
        return u

    lax.fori_loop(0, chunks + 2, step, 0)

    quarter = n_tok // n_t

    def zc(k):
        dev = lax.rem(t + k, n_t)
        return pltpu.make_async_remote_copy(
            src_ref=zs.at[k - 1], dst_ref=zr.at[k - 1],
            send_sem=z_s.at[k - 1], recv_sem=z_r.at[k - 1],
            device_id=(d, dev), device_id_type=MESH_ID,
        )

    def band(q):
        return pl.ds(pl.multiple_of(q * quarter, quarter), quarter)

    def za(k):
        dev = lax.rem(t + k, n_t)
        return pltpu.make_async_remote_copy(
            src_ref=gt.at[band(t)], dst_ref=gt.at[band(t)],
            send_sem=za_s.at[k - 1], recv_sem=za_r.at[k - 1],
            device_id=(d, dev), device_id_type=MESH_ID,
        )

    def za_in(k):
        dev = lax.rem(t + n_t - k, n_t)
        return pltpu.make_async_remote_copy(
            src_ref=gt.at[band(dev)], dst_ref=gt.at[band(dev)],
            send_sem=za_s.at[k - 1], recv_sem=za_r.at[k - 1],
            device_id=(d, dev), device_id_type=MESH_ID,
        )

    for k in range(1, n_t):
        dev = lax.rem(t + k, n_t)
        zs[k - 1] = acc[band(dev)].astype(BF16)
        zc(k).start()
    pair_sum(chunks - 1)
    lax.fori_loop(0, min(4, chunks), lambda j, u: (cross_sum(j), u)[1], 0)

    total = acc[band(t)]
    for k in range(1, n_t):
        zc(k).wait_recv()
        total += zr[k - 1].astype(F32)
    gt[band(t)] = total.astype(BF16)
    for k in range(1, n_t):
        za(k).start()
    lax.fori_loop(min(4, chunks), chunks, lambda j, u: (cross_sum(j), u)[1], 0)
    lax.fori_loop(0, chunks, lambda j, u: (finish(j), u)[1], 0)
    lax.fori_loop(0, chunks, lambda j, u: (drain(j), u)[1], 0)
    for k in range(1, n_t):
        zc(k).wait_send()
        za(k).wait_send()
        za_in(k).wait_recv()


def local_fused(n_dp, n_t, width, tokens, out_grad, gate_weight, up_weight, gate_mask, up_mask):
    n_tok, depth = tokens.shape
    rows, hidden_width = gate_weight.shape
    chunks = hidden_width // width
    half = rows // 2
    mask_rows = gate_mask.shape[0]
    gm = expand(gate_mask, mask_rows, hidden_width)
    um = expand(up_mask, mask_rows, hidden_width)
    vmem = pl.BlockSpec(memory_space=pltpu.VMEM)
    return pl.pallas_call(
        functools.partial(kernel, n_t, chunks, width, mask_rows),
        out_shape=(
            jax.ShapeDtypeStruct((n_tok, hidden_width), F32),
            jax.ShapeDtypeStruct((n_tok, depth), BF16),
            jax.ShapeDtypeStruct((rows, hidden_width), F32),
            jax.ShapeDtypeStruct((rows, hidden_width), F32),
        ),
        in_specs=[vmem] * 6,
        out_specs=(vmem,) * 4,
        scratch_shapes=[
            pltpu.VMEM((chunks, depth, 2 * width), BF16),
            pltpu.VMEM((chunks, n_dp // 2, rows, 2 * width), BF16),
            pltpu.VMEM((chunks, 2, half, 2 * width), BF16),
            pltpu.VMEM((chunks, 2, half, 2 * width), BF16),
            pltpu.VMEM((chunks, 2, half, 2 * width), BF16),
            pltpu.VMEM((depth, n_tok), BF16),
            pltpu.VMEM((n_tok, 2 * width), F32),
            pltpu.VMEM((n_tok, 2 * width), BF16),
            pltpu.VMEM((n_tok, depth), F32),
            pltpu.VMEM((n_t - 1, n_tok // n_t, depth), BF16),
            pltpu.VMEM((n_t - 1, n_tok // n_t, depth), BF16),
            pltpu.SemaphoreType.DMA((8, chunks)),
            pltpu.SemaphoreType.DMA((8, chunks)),
            pltpu.SemaphoreType.DMA((n_dp // 2, chunks)),
            pltpu.SemaphoreType.DMA((n_dp // 2, chunks)),
            pltpu.SemaphoreType.DMA((6, chunks)),
            pltpu.SemaphoreType.DMA((6, chunks)),
            pltpu.SemaphoreType.DMA((n_t - 1,)),
            pltpu.SemaphoreType.DMA((n_t - 1,)),
            pltpu.SemaphoreType.DMA((n_t - 1,)),
            pltpu.SemaphoreType.DMA((n_t - 1,)),
        ],
        compiler_params=pltpu.CompilerParams(
            collective_id=0, has_side_effects=True, vmem_limit_bytes=60 * 1024 * 1024
        ),
        cost_estimate=pl.CostEstimate(
            flops=12 * n_tok * depth * hidden_width,
            bytes_accessed=8 * n_tok * hidden_width,
            transcendentals=n_tok * hidden_width,
        ),
    )(tokens, out_grad, gate_weight, up_weight, gm, um)


def solution(mesh):
    placed = (
        P("dp", None),
        P("dp", "tensor"),
        P("dp", "tensor"),
        P("dp", "tensor"),
        P("dp", "tensor"),
        P("dp", "tensor"),
    )
    n_dp, n_t = mesh.shape["dp"], mesh.shape["tensor"]

    def local(tokens, out_grad, gate_weight, up_weight, gate_mask, up_mask):
        args = (tokens, out_grad, gate_weight, up_weight, gate_mask, up_mask)
        width = 256
        fits = (
            n_dp == 2 ** 3
            and n_t > 1
            and gate_weight.shape[1] % width == 0
            and gate_weight.shape[0] % 256 == 0
            and tokens.shape[0] % (16 * n_t) == 0
        )
        if fits:
            return local_fused(n_dp, n_t, width, *args)
        return local_collective(*args)

    return jax.shard_map(
        local,
        mesh=mesh,
        in_specs=placed,
        out_specs=(P("dp", "tensor"), P("dp", None), P("dp", "tensor"), P("dp", "tensor")),
        check_vma=False,
    )
```

```python
import functools

import jax
import jax.numpy as jnp
from jax import lax
from jax.experimental import pallas as pl
from jax.experimental.pallas import tpu as pltpu
from jax.sharding import PartitionSpec as P

MESH_ID = pl.DeviceIdType.MESH
F32 = jnp.float32
BF16 = jnp.bfloat16
LEAD = 3
EARLY = 2


def expand(block_mask, rows, columns):
    height, breadth = block_mask.shape
    down, across = rows // height, columns // breadth
    values = block_mask.astype(F32)
    return jnp.broadcast_to(
        values[:, None, :, None], (height, down, breadth, across)
    ).reshape(rows, columns)


def local_collective(tokens, out_grad, gate_weight, up_weight, gate_mask, up_mask):
    gate_keep = expand(gate_mask, *gate_weight.shape)
    up_keep = expand(up_mask, *up_weight.shape)
    gate_eff = gate_weight * gate_keep.astype(BF16)
    up_eff = up_weight * up_keep.astype(BF16)
    local_both = jnp.concatenate([gate_eff, up_eff], axis=1)
    hidden_width = gate_weight.shape[1]
    gathered = lax.all_gather(local_both, "dp", axis=0, tiled=True)
    preact = jnp.dot(tokens, gathered, preferred_element_type=F32)
    gate = preact[:, :hidden_width]
    up = preact[:, hidden_width:]
    sigmoid_gate = jax.nn.sigmoid(gate)
    activation = gate * sigmoid_gate
    hidden = activation * up
    grad_float = out_grad.astype(F32)
    d_gate = (grad_float * up * sigmoid_gate * (1.0 + gate * (1.0 - sigmoid_gate))).astype(BF16)
    d_up = (grad_float * activation).astype(BF16)
    d_both = jnp.concatenate([d_gate, d_up], axis=1)
    partial_input = lax.dot_general(
        d_both, gathered, (((1,), (1,)), ((), ())), preferred_element_type=F32
    )
    grad_tokens = lax.psum(partial_input, "tensor").astype(BF16)
    summed = lax.psum_scatter(
        lax.dot_general(
            tokens, d_both, (((0,), (0,)), ((), ())), preferred_element_type=F32
        ).astype(BF16),
        "dp",
        scatter_dimension=0,
        tiled=True,
    ).astype(F32)
    grad_gate = summed[:, :hidden_width] * gate_keep
    grad_up = summed[:, hidden_width:] * up_keep
    return (hidden, grad_tokens, grad_gate, grad_up)


def kernel(
    n_t, chunks, width, mask_rows,
    tok, og, gw, uw, gm, um,
    hidden, gt, ggrad, ugrad,
    wbuf, mr, xr, yr, r2, tokt, pre, dch, acc, zs, zr,
    ag_s, ag_r, ms_s, ms_r, rs_s, rs_r, z_s, z_r, za_s, za_r,
):
    rows = gw.shape[0]
    half = rows // 2
    n_tok, depth = tok.shape
    n_dp = depth // rows
    d = lax.axis_index("dp")
    t = lax.axis_index("tensor")
    c = lax.rem(d, 2)
    x = lax.rem(d // 2, 2)
    y = d // 4
    mate = d + 1 - 2 * c
    xn = d + 2 - 4 * x
    yn = d + 4 - 8 * y
    dg = xn + 4 - 8 * y

    barrier = pltpu.get_barrier_semaphore()
    for peer in (mate, xn, yn):
        pl.semaphore_signal(barrier, inc=1, device_id=(peer, t), device_id_type=MESH_ID)
    for k in range(1, n_t):
        pl.semaphore_signal(
            barrier, inc=1, device_id=(d, lax.rem(t + k, n_t)), device_id_type=MESH_ID
        )

    def at(j, block, off=0, size=rows):
        return wbuf.at[j, pl.ds(pl.multiple_of(block * rows + off, half), size)]

    def ag(kind, j):
        block, off, size, dev = (
            (d, 0, rows, xn),
            (d, 0, rows, yn),
            (xn, 0, half, yn),
            (yn, half, half, xn),
            (d, 0, rows, mate),
            (xn, 0, rows, mate),
            (yn, 0, rows, mate),
            (dg, 0, rows, mate),
        )[kind]
        return pltpu.make_async_remote_copy(
            src_ref=at(j, block, off, size), dst_ref=at(j, block, off, size),
            send_sem=ag_s.at[kind, j], recv_sem=ag_r.at[kind, j],
            device_id=(dev, t), device_id_type=MESH_ID,
        )

    def ag_in(kind, j):
        m = mate
        block, off, size = (
            (xn, 0, rows), (yn, 0, rows), (dg, 0, half), (dg, half, half),
            (m, 0, rows), (xn + m - d, 0, rows), (yn + m - d, 0, rows), (dg + m - d, 0, rows),
        )[kind]
        return pltpu.make_async_remote_copy(
            src_ref=at(j, block, off, size), dst_ref=at(j, block, off, size),
            send_sem=ag_s.at[kind, j], recv_sem=ag_r.at[kind, j],
            device_id=(mate, t), device_id_type=MESH_ID,
        )

    def ms(q, j):
        return pltpu.make_async_remote_copy(
            src_ref=at(j, 2 * q + 1 - c), dst_ref=mr.at[j, q],
            send_sem=ms_s.at[q, j], recv_sem=ms_r.at[q, j],
            device_id=(mate, t), device_id_type=MESH_ID,
        )

    def rs(kind, j):
        block, off, dst, dev = (
            (dg, 0, xr.at[j, 1], xn),
            (dg, half, yr.at[j, 1], yn),
            (xn, 0, xr.at[j, 0], xn),
            (yn, half, yr.at[j, 0], yn),
            (yn, 0, r2.at[j, 0], yn),
            (xn, half, r2.at[j, 1], xn),
        )[kind]
        return pltpu.make_async_remote_copy(
            src_ref=at(j, block, off, half), dst_ref=dst,
            send_sem=rs_s.at[kind, j], recv_sem=rs_r.at[kind, j],
            device_id=(dev, t), device_id_type=MESH_ID,
        )

    def cols(j):
        return pl.ds(pl.multiple_of(j * width, width), width)

    def keep(ref, j):
        down = rows // mask_rows
        return jnp.concatenate(
            [jnp.broadcast_to(ref[i:i + 1, cols(j)], (down, width)) for i in range(mask_rows)],
            axis=0,
        )

    def prepare(j):
        own = pl.ds(pl.multiple_of(d * rows, rows), rows)
        wbuf[j, own, :width] = (gw[:, cols(j)].astype(F32) * keep(gm, j)).astype(BF16)
        wbuf[j, own, width:] = (uw[:, cols(j)].astype(F32) * keep(um, j)).astype(BF16)

    def send_own(j):
        ag(0, j).start()
        ag(1, j).start()
        ag(4, j).start()

    prepare(0)
    pl.semaphore_wait(barrier, 3 + n_t - 1)
    lead = min(LEAD, chunks)

    def begin(j, u):
        @pl.when(j < lead)
        def _():
            send_own(j)

        @pl.when(j + 1 < chunks)
        def _():
            prepare(j + 1)

        return u

    lax.fori_loop(0, chunks, begin, 0)

    tokt[...] = tok[...].T
    acc[...] = jnp.zeros_like(acc)

    def relay(j):
        ag_in(0, j).wait_recv()
        ag(2, j).start()
        ag(5, j).start()
        ag_in(1, j).wait_recv()
        ag(3, j).start()
        ag(6, j).start()

        @pl.when(j + lead < chunks)
        def _():
            send_own(j + lead)

    def relay_far(j):
        ag_in(2, j).wait_recv()
        ag_in(3, j).wait_recv()
        ag(7, j).start()

    quarter = n_tok // n_t

    def zc(k):
        dev = lax.rem(t + k, n_t)
        return pltpu.make_async_remote_copy(
            src_ref=zs.at[k - 1], dst_ref=zr.at[k - 1],
            send_sem=z_s.at[k - 1], recv_sem=z_r.at[k - 1],
            device_id=(d, dev), device_id_type=MESH_ID,
        )

    def band(q):
        return pl.ds(pl.multiple_of(q * quarter, quarter), quarter)

    def za(k):
        dev = lax.rem(t + k, n_t)
        return pltpu.make_async_remote_copy(
            src_ref=gt.at[band(t)], dst_ref=gt.at[band(t)],
            send_sem=za_s.at[k - 1], recv_sem=za_r.at[k - 1],
            device_id=(d, dev), device_id_type=MESH_ID,
        )

    def za_in(k):
        dev = lax.rem(t + n_t - k, n_t)
        return pltpu.make_async_remote_copy(
            src_ref=gt.at[band(dev)], dst_ref=gt.at[band(dev)],
            send_sem=za_s.at[k - 1], recv_sem=za_r.at[k - 1],
            device_id=(d, dev), device_id_type=MESH_ID,
        )

    def send_input_terms():
        for k in range(1, n_t):
            zs[k - 1] = acc[band(lax.rem(t + k, n_t))].astype(BF16)
            zc(k).start()

    def compute(j):
        for kind in (4, 5, 6, 7):
            ag_in(kind, j).wait_recv()
        pre[...] = jnp.dot(tok[...], wbuf[j], preferred_element_type=F32)
        step = n_tok // 3 if n_tok % 48 == 0 else n_tok
        for i in range(0, n_tok, step):
            part = slice(i, i + step)
            gate = pre[part, :width]
            up = pre[part, width:]
            s = jax.nn.sigmoid(gate)
            activation = gate * s
            hidden[part, cols(j)] = (activation * up).astype(BF16)
            g = og[part, cols(j)].astype(F32)
            dch[part, :width] = (g * up * s * (1.0 + gate * (1.0 - s))).astype(BF16)
            dch[part, width:] = (g * activation).astype(BF16)
        for b in range(n_dp):
            acc[:, b * rows:(b + 1) * rows] += lax.dot_general(
                dch[...], wbuf[j, b * rows:(b + 1) * rows, :],
                (((1,), (1,)), ((), ())), preferred_element_type=F32,
            )

        @pl.when(j == chunks - 1)
        def _():
            send_input_terms()

        for kind in range(8):
            ag(kind, j).wait_send()
        for q in range(n_dp // 2):
            other = pl.ds(pl.multiple_of((2 * q + 1 - c) * rows, rows), rows)
            wbuf[j, other] = jnp.dot(
                tokt[other], dch[...], preferred_element_type=F32
            ).astype(BF16)
            ms(q, j).start()
        for q in range(n_dp // 2):
            mine = pl.ds(pl.multiple_of((2 * q + c) * rows, rows), rows)
            wbuf[j, mine] = jnp.dot(
                tokt[mine], dch[...], preferred_element_type=F32
            ).astype(BF16)

    def pair_sum(j):
        for q in range(n_dp // 2):
            mine = pl.ds(pl.multiple_of((2 * q + c) * rows, rows), rows)
            ms(q, j).wait_recv()
            wbuf[j, mine] = (wbuf[j, mine].astype(F32) + mr[j, q].astype(F32)).astype(BF16)
        for kind in range(4):
            rs(kind, j).start()

    def cross_sum(j):
        far = pl.ds(pl.multiple_of(yn * rows, rows), half)
        rs(0, j).wait_recv()
        wbuf[j, far] = (wbuf[j, far].astype(F32) + xr[j, 1].astype(F32)).astype(BF16)
        rs(4, j).start()
        far = pl.ds(pl.multiple_of(xn * rows + half, half), half)
        rs(1, j).wait_recv()
        wbuf[j, far] = (wbuf[j, far].astype(F32) + yr[j, 1].astype(F32)).astype(BF16)
        rs(5, j).start()

    def finish(j):
        for kind in (2, 3, 4, 5):
            rs(kind, j).wait_recv()
        for k, near in ((0, xr), (1, yr)):
            own = pl.ds(pl.multiple_of(d * rows + k * half, half), half)
            total = wbuf[j, own].astype(F32) + near[j, 0].astype(F32) + r2[j, k].astype(F32)
            part = slice(k * half, (k + 1) * half)
            ggrad[part, cols(j)] = (total[:, :width] * keep(gm, j)[part]).astype(BF16)
            ugrad[part, cols(j)] = (total[:, width:] * keep(um, j)[part]).astype(BF16)

    def drain(j):
        for q in range(n_dp // 2):
            ms(q, j).wait_send()
        for kind in range(6):
            rs(kind, j).wait_send()

    def when(stage, j):
        @pl.when(jnp.logical_and(j >= 0, j < chunks))
        def _():
            stage(j)

    def step(s, u):
        when(relay, s)
        when(relay_far, s - 1)
        when(compute, s - 2)
        when(pair_sum, s - 6)
        return u

    lax.fori_loop(0, chunks + 2, step, 0)

    lax.fori_loop(max(0, chunks - 4), chunks, lambda j, u: (pair_sum(j), u)[1], 0)

    def settle(j, u):
        when(cross_sum, j)
        when(finish, j - 2)
        return u

    early = min(EARLY, chunks)
    lax.fori_loop(0, early, settle, 0)
    total = acc[band(t)]
    for k in range(1, n_t):
        zc(k).wait_recv()
        total += zr[k - 1].astype(F32)
    gt[band(t)] = total.astype(BF16)
    for k in range(1, n_t):
        za(k).start()
    lax.fori_loop(early, chunks + 2, settle, 0)
    lax.fori_loop(0, chunks, lambda j, u: (drain(j), u)[1], 0)
    for k in range(1, n_t):
        zc(k).wait_send()
        za(k).wait_send()
        za_in(k).wait_recv()


def local_fused(n_dp, n_t, width, tokens, out_grad, gate_weight, up_weight, gate_mask, up_mask):
    n_tok, depth = tokens.shape
    rows, hidden_width = gate_weight.shape
    chunks = hidden_width // width
    half = rows // 2
    mask_rows = gate_mask.shape[0]
    gm = expand(gate_mask, mask_rows, hidden_width)
    um = expand(up_mask, mask_rows, hidden_width)
    vmem = pl.BlockSpec(memory_space=pltpu.VMEM)
    hidden, grad_tokens, grad_gate, grad_up = pl.pallas_call(
        functools.partial(kernel, n_t, chunks, width, mask_rows),
        out_shape=(
            jax.ShapeDtypeStruct((n_tok, hidden_width), BF16),
            jax.ShapeDtypeStruct((n_tok, depth), BF16),
            jax.ShapeDtypeStruct((rows, hidden_width), BF16),
            jax.ShapeDtypeStruct((rows, hidden_width), BF16),
        ),
        in_specs=[vmem] * 6,
        out_specs=(vmem,) * 4,
        scratch_shapes=[
            pltpu.VMEM((chunks, depth, 2 * width), BF16),
            pltpu.VMEM((chunks, n_dp // 2, rows, 2 * width), BF16),
            pltpu.VMEM((chunks, 2, half, 2 * width), BF16),
            pltpu.VMEM((chunks, 2, half, 2 * width), BF16),
            pltpu.VMEM((chunks, 2, half, 2 * width), BF16),
            pltpu.VMEM((depth, n_tok), BF16),
            pltpu.VMEM((n_tok, 2 * width), F32),
            pltpu.VMEM((n_tok, 2 * width), BF16),
            pltpu.VMEM((n_tok, depth), F32),
            pltpu.VMEM((n_t - 1, n_tok // n_t, depth), BF16),
            pltpu.VMEM((n_t - 1, n_tok // n_t, depth), BF16),
            pltpu.SemaphoreType.DMA((8, chunks)),
            pltpu.SemaphoreType.DMA((8, chunks)),
            pltpu.SemaphoreType.DMA((n_dp // 2, chunks)),
            pltpu.SemaphoreType.DMA((n_dp // 2, chunks)),
            pltpu.SemaphoreType.DMA((6, chunks)),
            pltpu.SemaphoreType.DMA((6, chunks)),
            pltpu.SemaphoreType.DMA((n_t - 1,)),
            pltpu.SemaphoreType.DMA((n_t - 1,)),
            pltpu.SemaphoreType.DMA((n_t - 1,)),
            pltpu.SemaphoreType.DMA((n_t - 1,)),
        ],
        compiler_params=pltpu.CompilerParams(
            collective_id=0, has_side_effects=True, vmem_limit_bytes=60 * 1024 * 1024
        ),
        cost_estimate=pl.CostEstimate(
            flops=12 * n_tok * depth * hidden_width,
            bytes_accessed=8 * n_tok * hidden_width,
            transcendentals=n_tok * hidden_width,
        ),
    )(tokens, out_grad, gate_weight, up_weight, gm, um)
    return hidden.astype(F32), grad_tokens, grad_gate.astype(F32), grad_up.astype(F32)


def solution(mesh):
    placed = (
        P("dp", None),
        P("dp", "tensor"),
        P("dp", "tensor"),
        P("dp", "tensor"),
        P("dp", "tensor"),
        P("dp", "tensor"),
    )
    n_dp, n_t = mesh.shape["dp"], mesh.shape["tensor"]

    def local(tokens, out_grad, gate_weight, up_weight, gate_mask, up_mask):
        args = (tokens, out_grad, gate_weight, up_weight, gate_mask, up_mask)
        width = 256
        fits = (
            n_dp == 2 ** 3
            and n_t > 1
            and gate_weight.shape[1] % width == 0
            and gate_weight.shape[0] % 256 == 0
            and tokens.shape[0] % (16 * n_t) == 0
        )
        if fits:
            return local_fused(n_dp, n_t, width, *args)
        return local_collective(*args)

    return jax.shard_map(
        local,
        mesh=mesh,
        in_specs=placed,
        out_specs=(P("dp", "tensor"), P("dp", None), P("dp", "tensor"), P("dp", "tensor")),
        check_vma=False,
    )
```

```python
import functools

import jax
import jax.numpy as jnp
from jax import lax
from jax.experimental import pallas as pl
from jax.experimental.pallas import tpu as pltpu
from jax.sharding import PartitionSpec as P

MESH_ID = pl.DeviceIdType.MESH
F32 = jnp.float32
BF16 = jnp.bfloat16
LEAD = 2
EARLY = 2


def expand(block_mask, rows, columns, kind=F32):
    height, breadth = block_mask.shape
    down, across = rows // height, columns // breadth
    values = block_mask.astype(kind)
    return jnp.broadcast_to(
        values[:, None, :, None], (height, down, breadth, across)
    ).reshape(rows, columns)


def local_collective(tokens, out_grad, gate_weight, up_weight, gate_mask, up_mask):
    gate_keep = expand(gate_mask, *gate_weight.shape)
    up_keep = expand(up_mask, *up_weight.shape)
    gate_eff = gate_weight * gate_keep.astype(BF16)
    up_eff = up_weight * up_keep.astype(BF16)
    local_both = jnp.concatenate([gate_eff, up_eff], axis=1)
    hidden_width = gate_weight.shape[1]
    gathered = lax.all_gather(local_both, "dp", axis=0, tiled=True)
    preact = jnp.dot(tokens, gathered, preferred_element_type=F32)
    gate = preact[:, :hidden_width]
    up = preact[:, hidden_width:]
    sigmoid_gate = jax.nn.sigmoid(gate)
    activation = gate * sigmoid_gate
    hidden = activation * up
    grad_float = out_grad.astype(F32)
    d_gate = (grad_float * up * sigmoid_gate * (1.0 + gate * (1.0 - sigmoid_gate))).astype(BF16)
    d_up = (grad_float * activation).astype(BF16)
    d_both = jnp.concatenate([d_gate, d_up], axis=1)
    partial_input = lax.dot_general(
        d_both, gathered, (((1,), (1,)), ((), ())), preferred_element_type=F32
    )
    grad_tokens = lax.psum(partial_input, "tensor").astype(BF16)
    summed = lax.psum_scatter(
        lax.dot_general(
            tokens, d_both, (((0,), (0,)), ((), ())), preferred_element_type=F32
        ).astype(BF16),
        "dp",
        scatter_dimension=0,
        tiled=True,
    ).astype(F32)
    grad_gate = summed[:, :hidden_width] * gate_keep
    grad_up = summed[:, hidden_width:] * up_keep
    return (hidden, grad_tokens, grad_gate, grad_up)


def kernel(
    n_t, chunks, width, mask_rows,
    tok, og, gw, uw, gm, um,
    hidden, gt, ggrad, ugrad,
    wbuf, mr, xr, yr, r2, tokt, pre, dch, acc, zs, zr,
    ag_s, ag_r, ms_s, ms_r, rs_s, rs_r, z_s, z_r, za_s, za_r,
):
    rows = gw.shape[0]
    half = rows // 2
    n_tok, depth = tok.shape
    n_dp = depth // rows
    d = lax.axis_index("dp")
    t = lax.axis_index("tensor")
    c = lax.rem(d, 2)
    x = lax.rem(d // 2, 2)
    y = d // 4
    mate = d + 1 - 2 * c
    xn = d + 2 - 4 * x
    yn = d + 4 - 8 * y
    dg = xn + 4 - 8 * y

    barrier = pltpu.get_barrier_semaphore()
    for peer in (mate, xn, yn):
        pl.semaphore_signal(barrier, inc=1, device_id=(peer, t), device_id_type=MESH_ID)
    for k in range(1, n_t):
        pl.semaphore_signal(
            barrier, inc=1, device_id=(d, lax.rem(t + k, n_t)), device_id_type=MESH_ID
        )

    def at(j, block, off=0, size=rows):
        return wbuf.at[j, pl.ds(pl.multiple_of(block * rows + off, half), size)]

    def ag(kind, j):
        block, off, size, dev = (
            (d, 0, rows, xn),
            (d, 0, rows, yn),
            (xn, 0, half, yn),
            (yn, half, half, xn),
            (d, 0, rows, mate),
            (xn, 0, rows, mate),
            (yn, 0, rows, mate),
            (dg, 0, rows, mate),
        )[kind]
        return pltpu.make_async_remote_copy(
            src_ref=at(j, block, off, size), dst_ref=at(j, block, off, size),
            send_sem=ag_s.at[kind, j], recv_sem=ag_r.at[kind, j],
            device_id=(dev, t), device_id_type=MESH_ID,
        )

    def ag_in(kind, j):
        m = mate
        block, off, size = (
            (xn, 0, rows), (yn, 0, rows), (dg, 0, half), (dg, half, half),
            (m, 0, rows), (xn + m - d, 0, rows), (yn + m - d, 0, rows), (dg + m - d, 0, rows),
        )[kind]
        return pltpu.make_async_remote_copy(
            src_ref=at(j, block, off, size), dst_ref=at(j, block, off, size),
            send_sem=ag_s.at[kind, j], recv_sem=ag_r.at[kind, j],
            device_id=(mate, t), device_id_type=MESH_ID,
        )

    def ms(q, j):
        return pltpu.make_async_remote_copy(
            src_ref=at(j, 2 * q + 1 - c), dst_ref=mr.at[j, q],
            send_sem=ms_s.at[q, j], recv_sem=ms_r.at[q, j],
            device_id=(mate, t), device_id_type=MESH_ID,
        )

    def rs(kind, j):
        block, off, dst, dev = (
            (dg, 0, xr.at[j, 1], xn),
            (dg, half, yr.at[j, 1], yn),
            (xn, 0, xr.at[j, 0], xn),
            (yn, half, yr.at[j, 0], yn),
            (yn, 0, r2.at[j, 0], yn),
            (xn, half, r2.at[j, 1], xn),
        )[kind]
        return pltpu.make_async_remote_copy(
            src_ref=at(j, block, off, half), dst_ref=dst,
            send_sem=rs_s.at[kind, j], recv_sem=rs_r.at[kind, j],
            device_id=(dev, t), device_id_type=MESH_ID,
        )

    def cols(j):
        return pl.ds(pl.multiple_of(j * width, width), width)

    def keep(ref, j):
        down = rows // mask_rows
        return jnp.concatenate(
            [
                jnp.broadcast_to(ref[i:i + 1, cols(j)].astype(F32), (down, width))
                for i in range(mask_rows)
            ],
            axis=0,
        )

    def prepare(j):
        own = pl.ds(pl.multiple_of(d * rows, rows), rows)
        wbuf[j, own, :width] = (gw[:, cols(j)].astype(F32) * keep(gm, j)).astype(BF16)
        wbuf[j, own, width:] = (uw[:, cols(j)].astype(F32) * keep(um, j)).astype(BF16)

    def send_own(j):
        ag(0, j).start()
        ag(1, j).start()
        ag(4, j).start()

    prepare(0)
    pl.semaphore_wait(barrier, 3 + n_t - 1)
    lead = min(LEAD, chunks)

    def begin(j, u):
        @pl.when(j < lead)
        def _():
            send_own(j)

        @pl.when(j + 1 < chunks)
        def _():
            prepare(j + 1)

        return u

    lax.fori_loop(0, chunks, begin, 0)

    tokt[...] = tok[...].T
    acc[...] = jnp.zeros_like(acc)

    def relay(j):
        ag_in(0, j).wait_recv()
        ag(2, j).start()
        ag(5, j).start()
        ag_in(1, j).wait_recv()
        ag(3, j).start()
        ag(6, j).start()

        @pl.when(j + lead < chunks)
        def _():
            send_own(j + lead)

    def relay_far(j):
        ag_in(2, j).wait_recv()
        ag_in(3, j).wait_recv()
        ag(7, j).start()

    quarter = n_tok // n_t

    def zc(k):
        dev = lax.rem(t + k, n_t)
        return pltpu.make_async_remote_copy(
            src_ref=zs.at[k - 1], dst_ref=zr.at[k - 1],
            send_sem=z_s.at[k - 1], recv_sem=z_r.at[k - 1],
            device_id=(d, dev), device_id_type=MESH_ID,
        )

    def band(q):
        return pl.ds(pl.multiple_of(q * quarter, quarter), quarter)

    def za(k):
        dev = lax.rem(t + k, n_t)
        return pltpu.make_async_remote_copy(
            src_ref=gt.at[band(t)], dst_ref=gt.at[band(t)],
            send_sem=za_s.at[k - 1], recv_sem=za_r.at[k - 1],
            device_id=(d, dev), device_id_type=MESH_ID,
        )

    def za_in(k):
        dev = lax.rem(t + n_t - k, n_t)
        return pltpu.make_async_remote_copy(
            src_ref=gt.at[band(dev)], dst_ref=gt.at[band(dev)],
            send_sem=za_s.at[k - 1], recv_sem=za_r.at[k - 1],
            device_id=(d, dev), device_id_type=MESH_ID,
        )

    def send_input_terms():
        for k in range(1, n_t):
            zs[k - 1] = acc[band(lax.rem(t + k, n_t))].astype(BF16)
            zc(k).start()

    def compute(j):
        for kind in (4, 5, 6, 7):
            ag_in(kind, j).wait_recv()
        pre[...] = jnp.dot(tok[...], wbuf[j], preferred_element_type=F32)
        step = n_tok // 3 if n_tok % 48 == 0 else n_tok
        for i in range(0, n_tok, step):
            part = slice(i, i + step)
            gate = pre[part, :width]
            up = pre[part, width:]
            s = jax.nn.sigmoid(gate)
            activation = gate * s
            hidden[part, cols(j)] = (activation * up).astype(BF16)
            g = og[part, cols(j)].astype(F32)
            dch[part, :width] = (g * up * s * (1.0 + gate * (1.0 - s))).astype(BF16)
            dch[part, width:] = (g * activation).astype(BF16)
        for b in range(n_dp):
            acc[:, b * rows:(b + 1) * rows] += lax.dot_general(
                dch[...], wbuf[j, b * rows:(b + 1) * rows, :],
                (((1,), (1,)), ((), ())), preferred_element_type=F32,
            )

        @pl.when(j == chunks - 1)
        def _():
            send_input_terms()

        for kind in range(8):
            ag(kind, j).wait_send()
        for q in range(n_dp // 2):
            other = pl.ds(pl.multiple_of((2 * q + 1 - c) * rows, rows), rows)
            wbuf[j, other] = jnp.dot(
                tokt[other], dch[...], preferred_element_type=F32
            ).astype(BF16)
            ms(q, j).start()
        for q in range(n_dp // 2):
            mine = pl.ds(pl.multiple_of((2 * q + c) * rows, rows), rows)
            wbuf[j, mine] = jnp.dot(
                tokt[mine], dch[...], preferred_element_type=F32
            ).astype(BF16)

    def pair_sum(j):
        for q in range(n_dp // 2):
            mine = pl.ds(pl.multiple_of((2 * q + c) * rows, rows), rows)
            ms(q, j).wait_recv()
            wbuf[j, mine] = (wbuf[j, mine].astype(F32) + mr[j, q].astype(F32)).astype(BF16)
        for kind in range(4):
            rs(kind, j).start()

    def cross_sum(j):
        far = pl.ds(pl.multiple_of(yn * rows, rows), half)
        rs(0, j).wait_recv()
        wbuf[j, far] = (wbuf[j, far].astype(F32) + xr[j, 1].astype(F32)).astype(BF16)
        rs(4, j).start()
        far = pl.ds(pl.multiple_of(xn * rows + half, half), half)
        rs(1, j).wait_recv()
        wbuf[j, far] = (wbuf[j, far].astype(F32) + yr[j, 1].astype(F32)).astype(BF16)
        rs(5, j).start()

    def finish(j):
        for kind in (2, 3, 4, 5):
            rs(kind, j).wait_recv()
        for k, near in ((0, xr), (1, yr)):
            own = pl.ds(pl.multiple_of(d * rows + k * half, half), half)
            total = wbuf[j, own].astype(F32) + near[j, 0].astype(F32) + r2[j, k].astype(F32)
            part = slice(k * half, (k + 1) * half)
            ggrad[part, cols(j)] = (total[:, :width] * keep(gm, j)[part]).astype(BF16)
            ugrad[part, cols(j)] = (total[:, width:] * keep(um, j)[part]).astype(BF16)

    def drain(j):
        for q in range(n_dp // 2):
            ms(q, j).wait_send()
        for kind in range(6):
            rs(kind, j).wait_send()

    def when(stage, j):
        @pl.when(jnp.logical_and(j >= 0, j < chunks))
        def _():
            stage(j)

    def step(s, u):
        when(relay, s)
        when(relay_far, s - 1)
        when(compute, s - 2)
        when(pair_sum, s - 6)
        return u

    lax.fori_loop(0, chunks + 2, step, 0)

    lax.fori_loop(max(0, chunks - 4), chunks, lambda j, u: (pair_sum(j), u)[1], 0)

    def settle(j, u):
        when(cross_sum, j)
        when(finish, j - 2)
        return u

    early = min(EARLY, chunks)
    lax.fori_loop(0, early, settle, 0)
    total = acc[band(t)]
    for k in range(1, n_t):
        zc(k).wait_recv()
        total += zr[k - 1].astype(F32)
    gt[band(t)] = total.astype(BF16)
    for k in range(1, n_t):
        za(k).start()
    lax.fori_loop(early, chunks + 2, settle, 0)
    lax.fori_loop(0, chunks, lambda j, u: (drain(j), u)[1], 0)
    for k in range(1, n_t):
        zc(k).wait_send()
        za(k).wait_send()
        za_in(k).wait_recv()


def local_fused(n_dp, n_t, width, tokens, out_grad, gate_weight, up_weight, gate_mask, up_mask):
    n_tok, depth = tokens.shape
    rows, hidden_width = gate_weight.shape
    chunks = hidden_width // width
    half = rows // 2
    mask_rows = gate_mask.shape[0]
    gm = expand(gate_mask, mask_rows, hidden_width, jnp.int32)
    um = expand(up_mask, mask_rows, hidden_width, jnp.int32)
    vmem = pl.BlockSpec(memory_space=pltpu.VMEM)
    hidden, grad_tokens, grad_gate, grad_up = pl.pallas_call(
        functools.partial(kernel, n_t, chunks, width, mask_rows),
        out_shape=(
            jax.ShapeDtypeStruct((n_tok, hidden_width), BF16),
            jax.ShapeDtypeStruct((n_tok, depth), BF16),
            jax.ShapeDtypeStruct((rows, hidden_width), BF16),
            jax.ShapeDtypeStruct((rows, hidden_width), BF16),
        ),
        in_specs=[vmem] * 6,
        out_specs=(vmem,) * 4,
        scratch_shapes=[
            pltpu.VMEM((chunks, depth, 2 * width), BF16),
            pltpu.VMEM((chunks, n_dp // 2, rows, 2 * width), BF16),
            pltpu.VMEM((chunks, 2, half, 2 * width), BF16),
            pltpu.VMEM((chunks, 2, half, 2 * width), BF16),
            pltpu.VMEM((chunks, 2, half, 2 * width), BF16),
            pltpu.VMEM((depth, n_tok), BF16),
            pltpu.VMEM((n_tok, 2 * width), F32),
            pltpu.VMEM((n_tok, 2 * width), BF16),
            pltpu.VMEM((n_tok, depth), F32),
            pltpu.VMEM((n_t - 1, n_tok // n_t, depth), BF16),
            pltpu.VMEM((n_t - 1, n_tok // n_t, depth), BF16),
            pltpu.SemaphoreType.DMA((8, chunks)),
            pltpu.SemaphoreType.DMA((8, chunks)),
            pltpu.SemaphoreType.DMA((n_dp // 2, chunks)),
            pltpu.SemaphoreType.DMA((n_dp // 2, chunks)),
            pltpu.SemaphoreType.DMA((6, chunks)),
            pltpu.SemaphoreType.DMA((6, chunks)),
            pltpu.SemaphoreType.DMA((n_t - 1,)),
            pltpu.SemaphoreType.DMA((n_t - 1,)),
            pltpu.SemaphoreType.DMA((n_t - 1,)),
            pltpu.SemaphoreType.DMA((n_t - 1,)),
        ],
        compiler_params=pltpu.CompilerParams(
            collective_id=0, has_side_effects=True, vmem_limit_bytes=60 * 1024 * 1024
        ),
        cost_estimate=pl.CostEstimate(
            flops=12 * n_tok * depth * hidden_width,
            bytes_accessed=8 * n_tok * hidden_width,
            transcendentals=n_tok * hidden_width,
        ),
    )(tokens, out_grad, gate_weight, up_weight, gm, um)
    return hidden.astype(F32), grad_tokens, grad_gate.astype(F32), grad_up.astype(F32)


def solution(mesh):
    placed = (
        P("dp", None),
        P("dp", "tensor"),
        P("dp", "tensor"),
        P("dp", "tensor"),
        P("dp", "tensor"),
        P("dp", "tensor"),
    )
    n_dp, n_t = mesh.shape["dp"], mesh.shape["tensor"]

    def local(tokens, out_grad, gate_weight, up_weight, gate_mask, up_mask):
        args = (tokens, out_grad, gate_weight, up_weight, gate_mask, up_mask)
        width = 256
        fits = (
            n_dp == 2 ** 3
            and n_t > 1
            and gate_weight.shape[1] % width == 0
            and gate_weight.shape[0] % 256 == 0
            and tokens.shape[0] % (16 * n_t) == 0
        )
        if fits:
            return local_fused(n_dp, n_t, width, *args)
        return local_collective(*args)

    return jax.shard_map(
        local,
        mesh=mesh,
        in_specs=placed,
        out_specs=(P("dp", "tensor"), P("dp", None), P("dp", "tensor"), P("dp", "tensor")),
        check_vma=False,
    )
```
